1024 devices in a mesh: wide: 32 (over z), narrow: 32 (over y, x, core).
Axes of the slice: x: 4, y: 4, z: 32, core: 2. Of those that a mesh axis runs over, the one named last changes fastest.
Arguments:
- tokens: bfloat16 [131072, 3584], P(('wide', 'narrow')), may hold values from -6 to 6
- cotangent: bfloat16 [131072, 3584], P(('wide', 'narrow')), may hold values from -6 to 6
- expert_ids: int32 [131072, 8], P(('wide', 'narrow')), may hold values from 0 to 383, as said below
- slots: int32 [131072, 8], P(('wide', 'narrow')), may hold values from 0 to 2, as said below
- probs: bfloat16 [131072, 8], P(('wide', 'narrow')), may hold values from 0.049804688 to 1
- w_gate: bfloat16 [3584, 8192], P('wide', 'narrow'), may hold values from -0.09375 to 0.09375
- w_up: bfloat16 [3584, 8192], P('wide', 'narrow'), may hold values from -0.09375 to 0.09375
- w_down: bfloat16 [8192, 3584], P('narrow', 'wide'), may hold values from -0.125 to 0.125
Outputs:
- token_grad: bfloat16 [131072, 3584], P(('wide', 'narrow'))
- prob_grad: float32 [131072, 8], P(('wide', 'narrow'))
The draws below stay inside these ranges and needn't reach their ends.
Inputs may be any that keep to these rules, and one draw needn't show every extreme that they name: `expert_ids`: each row names 8 different experts. Within the 128 rows of one device every expert below 4 is named by 1 to 3 rows, and in each group of 4096 tokens one such expert is named by exactly 3 rows on every device. Within the rows of one device, the choices that name one expert below 4 hold distinct slots.
All inputs are finite; a program needn't handle non-finite values.
Results may differ from the reference program's by a relative error of at most 0.019.
Values may be sent and summed in bfloat16 or wider, within the bound.
A program may use at most 32 MiB of HBM per device.

```python
import math
import jax
import jax.numpy as jnp
from jax import lax

D = 3584
FF = 2048
EXPERTS_ALL = 384
TOPK = 8
GROUP = 8
CAP = 3
TOK_DEV = 128
HID = 256
EXPERTS = 4
BLOCK = 4096
TOKENS = 131072
N_WIDE = 32
N_NARROW = 32


def route_tables(key):
    span = EXPERTS_ALL - EXPERTS
    group_count = TOKENS // BLOCK
    block_count = TOKENS // TOK_DEV
    hot_key = jax.random.fold_in(key, 7001)
    hot_group = jax.random.randint(hot_key, (group_count,), 0, EXPERTS)
    hot_block = jnp.repeat(hot_group, BLOCK // TOK_DEV, total_repeat_length=block_count)

    def one_block(block_key, hot_expert):
        subkeys = jax.random.split(block_key, 7)
        expert_range = jnp.arange(EXPERTS, dtype=jnp.int32)
        counts = jax.random.randint(subkeys[0], (EXPERTS,), 1, CAP + 1)
        counts = jnp.where(expert_range == hot_expert, CAP, counts)
        row_ids = jnp.arange(TOK_DEV, dtype=jnp.int32)
        owner = jnp.minimum(row_ids // CAP, EXPERTS - 1)
        within = row_ids % CAP
        holds = (row_ids < EXPERTS * CAP) & (within < counts[owner])
        window_id = jnp.where(holds, owner, -1)
        window_id = window_id[jax.random.permutation(subkeys[1], TOK_DEV)]
        base = jax.random.randint(subkeys[2], (TOK_DEV, 1), 0, span)
        stride = jax.random.randint(subkeys[3], (TOK_DEV, 1), 1, span // TOPK + 1)
        col_ids = jnp.arange(TOPK, dtype=jnp.int32)[None, :]
        others = EXPERTS + (base + col_ids * stride) % span
        chosen = jnp.where((col_ids == 0) & (window_id[:, None] >= 0), window_id[:, None], others)
        rotation = jax.random.randint(subkeys[4], (TOK_DEV, 1), 0, TOPK)
        chosen = jnp.take_along_axis(chosen, (col_ids + rotation) % TOPK, 1)
        onehot = (window_id[:, None] == expert_range[None, :]).astype(jnp.int32)
        ranking = jnp.cumsum(onehot, 0) - 1
        my_rank = jnp.sum(ranking * onehot, 1)
        offsets = jax.random.randint(subkeys[5], (EXPERTS,), 0, CAP)
        my_slot = (my_rank + offsets[jnp.maximum(window_id, 0)]) % CAP
        noise = jax.random.randint(subkeys[6], (TOK_DEV, TOPK), 0, CAP)
        slot_table = jnp.where(chosen < EXPERTS, my_slot[:, None], noise)
        return (chosen.astype(jnp.int32), slot_table.astype(jnp.int32))
    block_keys = jax.vmap(lambda number: jax.random.fold_in(key, number))(jnp.arange(block_count))
    chosen_all, slots_all = jax.vmap(one_block)(block_keys, hot_block)
    return (chosen_all.reshape(TOKENS, TOPK), slots_all.reshape(TOKENS, TOPK))


def draw_expert_ids(key, part):
    chosen_all, slots_all = route_tables(key)
    return chosen_all


def draw_slots(key, part):
    chosen_all, slots_all = route_tables(key)
    return slots_all


def level_of(stream_key, shape, cuts, low, top_value):
    gain = 1.0
    for axis_at, parts in cuts:
        steps = jax.random.uniform(jax.random.fold_in(jax.random.fold_in(stream_key, 6), axis_at), (parts,), jnp.float32, low / len(cuts), top_value / len(cuts))
        gain = gain * jnp.repeat(jnp.exp(steps), shape[axis_at] // parts).reshape((-1,) + (1,) * (len(shape) - 1 - axis_at))
    return gain


def bell_draw(key, extent, width, bound, pieces=(), held_as=jnp.bfloat16):
    factor_of = level_of(key, extent, pieces, -0.22, 0.18) if pieces else 1.0
    drawn = jax.random.normal(key, extent, jnp.float32) * width * factor_of
    return jnp.minimum(jnp.maximum(drawn, -bound), bound).astype(held_as)


def setup_inputs(seed: int = 0) -> dict:
    arg_keys = jax.random.split(jax.random.key(seed), 9)
    return {
        "tokens": bell_draw(arg_keys[0], (TOKENS, D), 1.0, 6.0, ((0, 1024),)),
        "cotangent": bell_draw(arg_keys[1], (TOKENS, D), 1.0, 6.0, ((0, 1024),)),
        "expert_ids": draw_expert_ids(jax.random.fold_in(arg_keys[8], 71), 0),
        "slots": draw_slots(jax.random.fold_in(arg_keys[8], 71), 0),
        "probs": jnp.clip(jnp.exp(math.log(1.0) - 2.9996462 * jax.random.uniform(arg_keys[4], (TOKENS, TOPK), jnp.float32) ** level_of(arg_keys[4], (TOKENS, TOPK), ((0, 1024),), -0.2, 0.2)), 0.049804688, 1.0).astype(jnp.bfloat16),
        "w_gate": bell_draw(arg_keys[5], (D, EXPERTS * FF), D ** -0.5, 0.09375, ((0, 32), (1, 32))),
        "w_up": bell_draw(arg_keys[6], (D, EXPERTS * FF), D ** -0.5, 0.09375, ((0, 32), (1, 32))),
        "w_down": bell_draw(arg_keys[7], (EXPERTS * FF, D), FF ** -0.5, 0.125, ((0, 32), (1, 32))),
    }


def silu_parts(values):
    sigma = jax.nn.sigmoid(values)
    return values * sigma, sigma * (1.0 + values * (1.0 - sigma))


def reference(tokens, cotangent, expert_ids, slots, probs, w_gate, w_up, w_down):
    slot_count = N_NARROW * CAP
    lanes_all = N_WIDE * EXPERTS * slot_count
    tok_index = jnp.arange(TOKENS, dtype=jnp.int32)
    device = tok_index // TOK_DEV
    group_index = device // N_NARROW
    sender = device % N_NARROW
    inside = expert_ids < EXPERTS
    flat_pos = jnp.where(inside, (group_index[:, None] * EXPERTS + expert_ids) * slot_count + sender[:, None] * CAP + slots, lanes_all).astype(jnp.int32)
    owners = jnp.broadcast_to(tok_index[:, None], flat_pos.shape).astype(jnp.int32)
    source = jnp.full((lanes_all,), TOKENS, jnp.int32).at[flat_pos.reshape(-1)].set(owners.reshape(-1), mode="drop")
    row_scale = jnp.zeros((lanes_all,), jnp.float32).at[flat_pos.reshape(-1)].set(probs.astype(jnp.float32).reshape(-1), mode="drop")
    zero_row = jnp.zeros((1, D), jnp.bfloat16)
    padded_x = jnp.concatenate([tokens, zero_row], 0)
    padded_dy = jnp.concatenate([cotangent, zero_row], 0)
    x_buffer = padded_x[source].reshape(N_WIDE, EXPERTS, slot_count, D)
    d_buffer = (row_scale[:, None] * padded_dy[source].astype(jnp.float32)).astype(jnp.bfloat16).reshape(N_WIDE, EXPERTS, slot_count, D)
    row_total = N_WIDE * slot_count

    def one_expert(expert):
        rows_x = x_buffer[:, expert].reshape(row_total, D)
        rows_d = d_buffer[:, expert].reshape(row_total, D)
        gate_w = lax.dynamic_slice_in_dim(w_gate, expert * FF, FF, 1)
        up_w = lax.dynamic_slice_in_dim(w_up, expert * FF, FF, 1)
        down_w = lax.dynamic_slice_in_dim(w_down, expert * FF, FF, 0)
        gate_act = jnp.dot(rows_x, gate_w, preferred_element_type=jnp.float32)
        up_act = jnp.dot(rows_x, up_w, preferred_element_type=jnp.float32)
        act, slope = silu_parts(gate_act)
        hidden = (act * up_act).astype(jnp.bfloat16)
        hid_blocks = hidden.astype(jnp.float32).reshape(row_total, GROUP, HID)
        down_blocks = down_w.astype(jnp.float32).reshape(GROUP, HID, D)
        partial_value = jnp.einsum("rgh,ghd->grd", hid_blocks, down_blocks).astype(jnp.bfloat16)
        partial_value = lax.optimization_barrier(partial_value)
        out_rows = jnp.sum(partial_value.astype(jnp.float32), 0)
        d_hidden = jnp.dot(rows_d, down_w.T, preferred_element_type=jnp.float32)
        d_gate = (d_hidden * up_act * slope).astype(jnp.bfloat16)
        d_up = (d_hidden * act).astype(jnp.bfloat16)
        dg_blocks = d_gate.astype(jnp.float32).reshape(row_total, GROUP, HID)
        du_blocks = d_up.astype(jnp.float32).reshape(row_total, GROUP, HID)
        wg_blocks = gate_w.astype(jnp.float32).reshape(D, GROUP, HID)
        wu_blocks = up_w.astype(jnp.float32).reshape(D, GROUP, HID)
        back = jnp.einsum("rgh,dgh->grd", dg_blocks, wg_blocks) + jnp.einsum("rgh,dgh->grd", du_blocks, wu_blocks)
        back = lax.optimization_barrier(back.astype(jnp.bfloat16))
        back_rows = jnp.sum(back.astype(jnp.float32), 0)
        return out_rows.reshape(N_WIDE, slot_count, D), back_rows.reshape(N_WIDE, slot_count, D)

    out_all, back_all = lax.map(one_expert, jnp.arange(EXPERTS, dtype=jnp.int32))
    zero_wide = jnp.zeros((1, D), jnp.float32)
    out_pad = jnp.concatenate([out_all.transpose(1, 0, 2, 3).reshape(lanes_all, D), zero_wide], 0)
    back_pad = jnp.concatenate([back_all.transpose(1, 0, 2, 3).reshape(lanes_all, D), zero_wide], 0)

    token_grad = jnp.zeros((TOKENS, D), jnp.float32)
    dy_wide = cotangent.astype(jnp.float32)
    grads = []
    for choice_pos in range(TOPK):
        index_k = flat_pos[:, choice_pos]
        live = inside[:, choice_pos].astype(jnp.float32)
        rows_out = out_pad[index_k]
        token_grad = token_grad + back_pad[index_k]
        grads.append(jnp.sum(dy_wide * rows_out, -1) * live)
    prob_grad = jnp.stack(grads, 1)
    return token_grad.astype(jnp.bfloat16), prob_grad
```

```python
import functools

import jax
import jax.numpy as jnp
from jax import lax
from jax.experimental import pallas as pl
from jax.experimental.pallas import tpu as pltpu
from jax.sharding import PartitionSpec as P

MESH = pl.DeviceIdType.MESH
F32 = jnp.float32
BF16 = jnp.bfloat16

NZ = 32
NP = 32
EXP = 4
PER_EXP = 8
TOK = 128
D = 3584
HID = 256
SH = 112
NQ = 4
QW = D // NQ
ROWS = NP * 4
HALF = NZ // 2


def place(n):
    return lax.rem(n, 2) * (NP // 2) + n // 2


def kernel(
    tok_hbm, cot_hbm, ids_ref, slots_ref, probs_ref, wg_hbm, wu_hbm, wd_ref,
    grad_ref, prob_ref,
    wbuf, tok, cot, msg, xin, xq, acc, dxs, outb, rin,
    loc_sem, ring_send, ring_recv, x_send, x_recv, r_send, r_recv,
):
    w = lax.axis_index("wide")
    n = lax.axis_index("narrow")
    right, left = lax.rem(w + 1, NZ), lax.rem(w + NZ - 1, NZ)
    my_place = place(n)
    my_exp = n // PER_EXP

    def load(i, src, dst):
        return pltpu.make_async_copy(src, dst, loc_sem.at[i])

    def rows_of(shard):
        return pl.ds(pl.multiple_of(shard * SH, 16), SH)

    loads = [
        load(0, wg_hbm, wbuf.at[0, rows_of(w)]),
        load(1, wu_hbm, wbuf.at[1, rows_of(w)]),
        load(2, tok_hbm, tok),
        load(3, cot_hbm, cot),
    ]
    for one in loads:
        one.start()

    barrier = pltpu.get_barrier_semaphore()

    def greet(d, carry):
        pl.semaphore_signal(barrier, inc=1, device_id=(w, lax.rem(n + d, NP)), device_id_type=MESH)
        return carry

    pl.semaphore_signal(barrier, inc=1, device_id=(left, n), device_id_type=MESH)
    pl.semaphore_signal(barrier, inc=1, device_id=(right, n), device_id_type=MESH)
    lax.fori_loop(1, NP, greet, 0)
    pl.semaphore_wait(barrier, NP + 1)

    def sem_at(way, k, c):
        return (way * (HALF + 1) + k) * 3 + c

    def hop(way, k, c, lo=0, size=SH, src=None):
        if way == 0:
            shard, to = lax.rem(w + NZ + 1 - k, NZ), right
        else:
            shard, to = lax.rem(w + NZ - 1 + k, NZ), left
        span = pl.ds(pl.multiple_of(shard * SH + lo, 16), size)
        here = wbuf.at[c, span]
        return pltpu.make_async_remote_copy(
            src_ref=here if src is None else src,
            dst_ref=here,
            send_sem=ring_send.at[sem_at(way, k, c)],
            recv_sem=ring_recv.at[sem_at(way, k, c)],
            device_id=(to, n),
            device_id_type=MESH,
        )

    def landed(way, k, c, lo=0, size=SH):
        shard = lax.rem(w + NZ - k, NZ) if way == 0 else lax.rem(w + k, NZ)
        here = wbuf.at[c, pl.ds(pl.multiple_of(shard * SH + lo, 16), size)]
        return pltpu.make_async_remote_copy(
            src_ref=here,
            dst_ref=here,
            send_sem=ring_send.at[sem_at(way, k, c)],
            recv_sem=ring_recv.at[sem_at(way, k, c)],
            device_id=(right, n),
            device_id_type=MESH,
        )

    for c, src in ((0, wg_hbm), (1, wu_hbm)):
        for way in (0, 1):
            hop(way, 1, c, src=src).start()
    eye = (
        lax.broadcasted_iota(jnp.int32, (SH, SH), 0) == lax.broadcasted_iota(jnp.int32, (SH, SH), 1)
    ).astype(F32).astype(BF16)
    wbuf[2, rows_of(w), :] = lax.dot_general(
        eye, wd_ref[...], (((1,), (1,)), ((), ())), preferred_element_type=F32
    ).astype(BF16)
    for way in (0, 1):
        hop(way, 1, 2).start()

    ids = ids_ref[...]
    target = jnp.where(ids < EXP, ids * 4 + slots_ref[...], -1)
    lane = lax.broadcasted_iota(jnp.int32, (TOK, 128), 1)
    code = jnp.where(lane < 64, (lane // 16) * 4 + lax.rem(lane, 4), -2)
    picks = jnp.zeros((TOK, 128), F32)
    for k in range(8):
        picks = picks + jnp.where(target[:, k : k + 1] == code, 1.0, 0.0)
    picks = jnp.transpose(picks)[:64].astype(BF16)
    row_q = lax.rem(lax.broadcasted_iota(jnp.int32, (64, QW), 0) // 4, NQ)
    loads[2].wait()
    loads[3].wait()
    for a, src in ((0, tok), (1, cot)):
        rows = jnp.zeros((64, QW), F32)
        for q in range(NQ):
            part = jnp.dot(picks, src[:, q * QW : (q + 1) * QW], preferred_element_type=F32)
            rows = jnp.where(row_q == q, part, rows)
        for e in range(EXP):
            msg[e, a] = rows[e * 16 : (e + 1) * 16].astype(BF16)

    def x_copy(d):
        dest = lax.rem(n + d, NP)
        return pltpu.make_async_remote_copy(
            src_ref=msg.at[dest // PER_EXP],
            dst_ref=xin.at[:, my_place],
            send_sem=x_send.at[d],
            recv_sem=x_recv.at[my_place],
            device_id=(w, dest),
            device_id_type=MESH,
        )

    def x_landed(d):
        origin = place(lax.rem(n + d, NP))
        return pltpu.make_async_remote_copy(
            src_ref=msg.at[0],
            dst_ref=xin.at[:, origin],
            send_sem=x_send.at[d],
            recv_sem=x_recv.at[origin],
            device_id=(w, n),
            device_id_type=MESH,
        )

    def x_start(d, carry):
        x_copy(d).start()
        return carry

    lax.fori_loop(1, NP, x_start, 0)
    own_x = load(4, msg.at[my_exp], xin.at[:, my_place])
    own_x.start()
    acc[...] = jnp.zeros_like(acc)
    own_x.wait()
    loads[0].wait()
    loads[1].wait()

    def step(k):
        for c in range(3):
            for way in (0, 1):
                landed(way, k, c).wait_recv()
                hop(way, k + 1, c).start()

    def steps(lo, hi, more=None):
        def body(k, carry):
            step(k)
            if more is not None:
                more(k)
            return carry

        lax.fori_loop(lo, hi, body, 0)

    steps(1, 8)

    def x_wait(d, carry):
        x_landed(d).wait_recv()
        return carry

    lax.fori_loop(1, NP, x_wait, 0)

    low = lax.broadcasted_iota(jnp.int32, (8, QW), 0) < 4

    def sort_rows(unit):
        a, g = unit // 8, lax.rem(unit, 8)
        block = [xin[a, 4 * g + i].astype(F32) for i in range(4)]
        for half in range(2):
            v = [one[half * 8 : half * 8 + 8] for one in block]
            r = [pltpu.roll(one, 4, 0) for one in v]
            even = [jnp.where(low, v[0], r[1]), jnp.where(low, v[2], r[3])]
            odd = [jnp.where(low, r[0], v[1]), jnp.where(low, r[2], v[3])]
            span = pl.ds(pl.multiple_of(g * 16, 16), 16)
            xq[a, 2 * half, span, :] = jnp.concatenate(even, 0).astype(BF16)
            xq[a, 2 * half + 1, span, :] = jnp.concatenate(odd, 0).astype(BF16)

    def sort_some(k):
        for i in range(4):
            sort_rows((k - 8) * 4 + i)

    steps(8, 12, sort_some)

    def group(j):
        span = pl.ds(pl.multiple_of(j * QW, 16), QW)
        for c in range(3):
            acc[c] += jnp.dot(xq[c // 2, j], wbuf[c, span, :], preferred_element_type=F32)

    j, r = w // 8, lax.rem(w, 8)
    near = lax.rem(j + jnp.where(r <= 3, 3, 1), 4)
    far = lax.rem(j + jnp.where(r <= 3, 1, 3), 4)
    group(j)
    steps(12, 13)
    group(near)
    steps(13, 15)
    last = ((0, 0, 0, SH), (1, 1, 0, SH), (0, 2, 0, 64), (1, 2, 64, 48))
    for c in range(3):
        for way in (0, 1):
            landed(way, HALF - 1, c).wait_recv()
            for way_l, c_l, lo, size in last:
                if (way_l, c_l) == (way, c):
                    hop(way, HALF, c, lo, size).start()
    group(far)
    for way, c, lo, size in last:
        landed(way, HALF, c, lo, size).wait_recv()
    group(lax.rem(j + 2, 4))

    gate, up, raw = acc[0], acc[1], acc[2]
    sigma = 1.0 / (1.0 + jnp.exp(-gate))
    act = gate * sigma
    slope = sigma * (1.0 + gate * (1.0 - sigma))
    d_gate = (raw * up * slope).astype(BF16)
    d_up = (raw * act).astype(BF16)
    score = jnp.sum(act * up * raw, axis=1, keepdims=True)

    row = lax.broadcasted_iota(jnp.int32, (ROWS, 128), 0)
    col = lax.broadcasted_iota(jnp.int32, (ROWS, 128), 1)
    slot = lax.rem(row, 4)
    high = score.astype(BF16).astype(F32)
    marks = jnp.where(col == slot, high, 0.0) + jnp.where(col == slot + 8, score - high, 0.0)
    marks = marks + pltpu.roll(marks, 1, 0)
    marks = marks + pltpu.roll(marks, 2, 0)
    marks = jnp.where(slot == 3, marks, 0.0)

    nt = (((1,), (1,)), ((), ()))
    for q in range(NQ):
        span = pl.ds(q * QW, QW)
        dxs[q] = lax.dot_general(d_gate, wbuf[0, span, :], nt, preferred_element_type=F32) + lax.dot_general(
            d_up, wbuf[1, span, :], nt, preferred_element_type=F32
        )
    dxs[0, :, 0:128] += marks

    def pack_rows(g, carry):
        for i in range(2):
            span = pl.ds(pl.multiple_of(g * 16 + i * 8, 8), 8)
            v = [dxs[q, span, :] for q in range(NQ)]
            r = [pltpu.roll(one, 4, 0) for one in v]
            first = [jnp.where(low, v[0], r[1]), jnp.where(low, v[2], r[3])]
            second = [jnp.where(low, r[0], v[1]), jnp.where(low, r[2], v[3])]
            outb[4 * g + 2 * i] = jnp.concatenate(first, 0).astype(BF16)
            outb[4 * g + 2 * i + 1] = jnp.concatenate(second, 0).astype(BF16)
        return carry

    lax.fori_loop(0, NP // 4, pack_rows, 0)

    def r_copy(d):
        dest = lax.rem(n + d, NP)
        return pltpu.make_async_remote_copy(
            src_ref=outb.at[place(dest)],
            dst_ref=rin.at[my_place],
            send_sem=r_send.at[d],
            recv_sem=r_recv.at[my_place],
            device_id=(w, dest),
            device_id_type=MESH,
        )

    def r_landed(d):
        origin = place(lax.rem(n + d, NP))
        return pltpu.make_async_remote_copy(
            src_ref=outb.at[0],
            dst_ref=rin.at[origin],
            send_sem=r_send.at[d],
            recv_sem=r_recv.at[origin],
            device_id=(w, n),
            device_id_type=MESH,
        )

    def r_start(d, carry):
        r_copy(d).start()
        return carry

    lax.fori_loop(1, NP, r_start, 0)
    own_r = load(5, outb.at[my_place], rin.at[my_place])
    own_r.start()

    lanes = NP * 16
    lane = lax.broadcasted_iota(jnp.int32, (TOK, lanes), 1)
    code = (lax.rem(lane // 16, NP // 2) // 4) * 4 + lax.rem(lane, 4)
    lane_q = lax.rem(lane // 4, NQ)
    probs = probs_ref[...].astype(F32)
    spread = jnp.zeros((TOK, lanes), F32)
    for k in range(8):
        spread = spread + jnp.where(target[:, k : k + 1] == code, probs[:, k : k + 1], 0.0)
    own_r.wait()

    def r_wait(d, carry):
        r_landed(d).wait_recv()
        return carry

    lax.fori_loop(1, NP, r_wait, 0)
    for q in range(NQ):
        mix = jnp.where(lane_q == q, spread, 0.0).astype(BF16)
        total = jnp.zeros((TOK, QW), F32)
        total = jnp.dot(mix, rin[...].reshape(lanes, QW), preferred_element_type=F32)
        grad_ref[:, q * QW : (q + 1) * QW] = total.astype(BF16)

    s_row = lax.broadcasted_iota(jnp.int32, (16, lanes), 0)
    s_col = lax.broadcasted_iota(jnp.int32, (16, lanes), 1)
    take = (lax.rem(s_col, 16) == 3) & (lax.rem(s_col // 16, NP // 2) // 4 == s_row)
    sums = jnp.dot(
        jnp.where(take, 1.0, 0.0).astype(BF16),
        rin[:, :, 0:128].reshape(lanes, 128),
        preferred_element_type=F32,
    )
    result = jnp.zeros((TOK, 8), F32)
    for e in range(EXP):
        for s in range(3):
            value = sums[e : e + 1, s : s + 1] + sums[e : e + 1, s + 8 : s + 9]
            result = jnp.where(target == e * 4 + s, value, result)
    prob_ref[...] = result

    def ring_done(k, carry):
        for c in range(3):
            for way in (0, 1):
                hop(way, k, c).wait_send()
        return carry

    lax.fori_loop(1, HALF, ring_done, 0)
    for way, c, lo, size in last:
        hop(way, HALF, c, lo, size).wait_send()

    def sends_done(d, carry):
        x_copy(d).wait_send()
        r_copy(d).wait_send()
        return carry

    lax.fori_loop(1, NP, sends_done, 0)


def shards(tokens, cotangent, expert_ids, slots, probs, w_gate, w_up, w_down):
    any_spec = pl.BlockSpec(memory_space=pl.ANY)
    vmem = pl.BlockSpec(memory_space=pltpu.VMEM)
    ring_sems = 2 * (HALF + 1) * 3
    return pl.pallas_call(
        kernel,
        out_shape=(
            jax.ShapeDtypeStruct((TOK, D), BF16),
            jax.ShapeDtypeStruct((TOK, 8), F32),
        ),
        in_specs=[any_spec, any_spec, vmem, vmem, vmem, any_spec, any_spec, vmem],
        out_specs=(vmem, vmem),
        scratch_shapes=[
            pltpu.VMEM((3, D, HID), BF16),
            pltpu.VMEM((TOK, D), BF16),
            pltpu.VMEM((TOK, D), BF16),
            pltpu.VMEM((EXP, 2, 16, QW), BF16),
            pltpu.VMEM((2, NP, 16, QW), BF16),
            pltpu.VMEM((2, NQ, ROWS, QW), BF16),
            pltpu.VMEM((3, ROWS, HID), F32),
            pltpu.VMEM((NQ, ROWS, QW), F32),
            pltpu.VMEM((NP, 16, QW), BF16),
            pltpu.VMEM((NP, 16, QW), BF16),
            pltpu.SemaphoreType.DMA((6,)),
            pltpu.SemaphoreType.DMA((ring_sems,)),
            pltpu.SemaphoreType.DMA((ring_sems,)),
            pltpu.SemaphoreType.DMA((NP,)),
            pltpu.SemaphoreType.DMA((NP,)),
            pltpu.SemaphoreType.DMA((NP,)),
            pltpu.SemaphoreType.DMA((NP,)),
        ],
        compiler_params=pltpu.CompilerParams(
            collective_id=0, has_side_effects=True, vmem_limit_bytes=56 * 1024 * 1024
        ),
    )(tokens, cotangent, expert_ids, slots, probs, w_gate, w_up, w_down)


def solution(mesh):
    rows = P(("wide", "narrow"), None)
    in_specs = (rows, rows, rows, rows, rows, P("wide", "narrow"), P("wide", "narrow"), P("narrow", "wide"))
    return jax.shard_map(shards, mesh=mesh, in_specs=in_specs, out_specs=(rows, rows), check_vma=False)
```

```python
import functools

import jax
import jax.numpy as jnp
from jax import lax
from jax.experimental import pallas as pl
from jax.experimental.pallas import tpu as pltpu
from jax.sharding import PartitionSpec as P

MESH = pl.DeviceIdType.MESH
F32 = jnp.float32
BF16 = jnp.bfloat16

NZ = 32
NP = 32
EXP = 4
PER_EXP = 8
TOK = 128
D = 3584
HID = 256
SH = 112
NQ = 4
QW = D // NQ
LANES = NP * 8
ROWS = NP * 4
HALF = NZ // 2
TURNS = ((0, 0), (1, 2), (0, 1), (1, 1), (0, 2), (1, 0))
CUTS = ((0, 512), (512, 384))


def place(n):
    return lax.rem(n, 2) * (NP // 2) + n // 2


def target_of(ids_ref, slots_ref):
    ids = ids_ref[...]
    return jnp.where(ids < EXP, ids * 4 + slots_ref[...], -1)


def one_hot(target, code, value=None):
    total = jnp.zeros(code.shape, F32)
    for k in range(8):
        held = 1.0 if value is None else value[k : k + 1]
        total = total + jnp.where(target[k : k + 1] == code, held, 0.0)
    return total


def kernel(
    tok_hbm, cot_hbm, ids_ref, slots_ref, probs_ref, wg_hbm, wu_hbm, wd_hbm,
    rin_a, rin_b, spread_ref,
    wbuf, tok, cot, msg, xin, xq, acc, dxs, give_a, give_b, took_a, took_b, out_a, out_b,
    loc_sem, ring_send, ring_recv, x_send, x_recv, c_send, c_recv, r_send, r_recv, word,
):
    w = lax.axis_index("wide")
    n = lax.axis_index("narrow")
    right, left = lax.rem(w + 1, NZ), lax.rem(w + NZ - 1, NZ)
    my_place = place(n)
    my_exp = n // PER_EXP

    def load(i, src, dst):
        return pltpu.make_async_copy(src, dst, loc_sem.at[i])

    def rows_of(shard):
        return pl.ds(pl.multiple_of(shard * SH, 16), SH)

    loads = [
        load(0, wg_hbm, wbuf.at[0, rows_of(w)]),
        load(1, wu_hbm, wbuf.at[1, rows_of(w)]),
        load(6, wd_hbm, wbuf.at[2, rows_of(w)]),
        load(2, tok_hbm, tok),
        load(3, cot_hbm, cot),
    ]
    for one in loads:
        one.start()

    core, chip = lax.rem(n, 2), n // 2
    side = 4 * (chip // 4)
    sibling = chip * 2 + 1 - core
    beside = [(side + lax.rem(chip + d, 4)) * 2 + core for d in (1, 3)]
    above = [lax.rem(chip + d, NP // 2) * 2 + core for d in (4, 12)]
    barrier = pltpu.get_barrier_semaphore()
    for to in [(left, n), (right, n), (w, sibling)] + [(w, one) for one in beside + above]:
        pl.semaphore_signal(barrier, inc=1, device_id=to, device_id_type=MESH)
    pl.semaphore_wait(barrier, 7)

    def tell(i, whom):
        for one in whom:
            pl.semaphore_signal(word.at[i], inc=1, device_id=(w, one), device_id_type=MESH)

    def hear(i, whom):
        pl.semaphore_wait(word.at[i], len(whom))

    tell(0, beside)

    def sem_at(way, k, c):
        return (way * (HALF + 1) + k) * 3 + c

    def hop(way, k, c, lo=0, size=SH, src=None):
        if way == 0:
            shard, to = lax.rem(w + NZ + 1 - k, NZ), right
        else:
            shard, to = lax.rem(w + NZ - 1 + k, NZ), left
        span = pl.ds(pl.multiple_of(shard * SH + lo, 16), size)
        here = wbuf.at[c, span]
        return pltpu.make_async_remote_copy(
            src_ref=here if src is None else src,
            dst_ref=here,
            send_sem=ring_send.at[sem_at(way, k, c)],
            recv_sem=ring_recv.at[sem_at(way, k, c)],
            device_id=(to, n),
            device_id_type=MESH,
        )

    def landed(way, k, c, lo=0, size=SH):
        shard = lax.rem(w + NZ - k, NZ) if way == 0 else lax.rem(w + k, NZ)
        here = wbuf.at[c, pl.ds(pl.multiple_of(shard * SH + lo, 16), size)]
        return pltpu.make_async_remote_copy(
            src_ref=here,
            dst_ref=here,
            send_sem=ring_send.at[sem_at(way, k, c)],
            recv_sem=ring_recv.at[sem_at(way, k, c)],
            device_id=(right, n),
            device_id_type=MESH,
        )

    for way, c in TURNS:
        hop(way, 1, c, src=(wg_hbm, wu_hbm, wd_hbm)[c]).start()

    def step(k):
        for way, c in TURNS:
            landed(way, k, c).wait_recv()
            hop(way, k + 1, c).start()

    def sent(k):
        for c in range(3):
            for way in (0, 1):
                hop(way, k, c).wait_send()

    def steps(lo, hi, more=None):
        def body(k, carry):
            step(k)
            if lo >= 2:
                sent(k - 1)
            if more is not None:
                more(k)
            return carry

        lax.fori_loop(lo, hi, body, 0)

    target = target_of(ids_ref, slots_ref)
    row = lax.broadcasted_iota(jnp.int32, (64, TOK), 0)
    picks = one_hot(target, (row // 16) * 4 + lax.rem(row, 4)).astype(BF16)
    row_q = lax.rem(lax.broadcasted_iota(jnp.int32, (64, QW), 0) // 4, NQ)

    def pick_rows(a, src):
        rows = jnp.zeros((64, QW), F32)
        for q in range(NQ):
            part = jnp.dot(picks, src[:, q * QW : (q + 1) * QW], preferred_element_type=F32)
            rows = jnp.where(row_q == q, part, rows)
        for e in range(EXP):
            msg[e, a] = rows[e * 16 : (e + 1) * 16].astype(BF16)

    def x_copy(d):
        dest = lax.rem(n + d, NP)
        return pltpu.make_async_remote_copy(
            src_ref=msg.at[dest // PER_EXP],
            dst_ref=xin.at[:, my_place],
            send_sem=x_send.at[d],
            recv_sem=x_recv.at[my_place],
            device_id=(w, dest),
            device_id_type=MESH,
        )

    def x_landed(d):
        origin = place(lax.rem(n + d, NP))
        return pltpu.make_async_remote_copy(
            src_ref=msg.at[0],
            dst_ref=xin.at[:, origin],
            send_sem=x_send.at[d],
            recv_sem=x_recv.at[origin],
            device_id=(w, n),
            device_id_type=MESH,
        )

    def x_start(d, carry):
        x_copy(d).start()
        return carry

    loads[3].wait()
    pick_rows(0, tok)
    hear(0, beside)
    tell(1, beside)
    steps(1, 2)
    hear(1, beside)
    tell(2, above)
    loads[4].wait()
    pick_rows(1, cot)
    hear(2, above)
    tell(3, [sibling])
    steps(2, 3)
    hear(3, [sibling])
    lax.fori_loop(1, 11, x_start, 0)
    steps(3, 4)
    lax.fori_loop(11, 21, x_start, 0)
    steps(4, 5)
    lax.fori_loop(21, NP, x_start, 0)
    own_x = load(4, msg.at[my_exp], xin.at[:, my_place])
    own_x.start()
    steps(5, 6)
    row = lax.broadcasted_iota(jnp.int32, (LANES, TOK), 0)
    spread_ref[...] = jnp.transpose(
        one_hot(target, (row // 64) * 4 + lax.rem(row, 4), probs_ref[...].astype(F32))
    ).astype(BF16)
    acc[...] = jnp.zeros_like(acc)
    own_x.wait()
    for one in loads[:3]:
        one.wait()
    steps(6, 9)

    def x_done(d, carry):
        x_copy(d).wait_send()
        return carry

    lax.fori_loop(1, NP, x_done, 0)

    def x_wait(d, carry):
        x_landed(d).wait_recv()
        return carry

    lax.fori_loop(1, NP, x_wait, 0)

    low = lax.broadcasted_iota(jnp.int32, (8, QW), 0) < 4

    def sort_rows(unit):
        a, g = unit // 8, lax.rem(unit, 8)
        block = [xin[a, 4 * g + i].astype(F32) for i in range(4)]
        for half in range(2):
            v = [one[half * 8 : half * 8 + 8] for one in block]
            r = [pltpu.roll(one, 4, 0) for one in v]
            even = [jnp.where(low, v[0], r[1]), jnp.where(low, v[2], r[3])]
            odd = [jnp.where(low, r[0], v[1]), jnp.where(low, r[2], v[3])]
            span = pl.ds(pl.multiple_of(g * 16, 16), 16)
            xq[a, 2 * half, span, :] = jnp.concatenate(even, 0).astype(BF16)
            xq[a, 2 * half + 1, span, :] = jnp.concatenate(odd, 0).astype(BF16)

    def sort_some(k):
        for i in range(4):
            sort_rows((k - 9) * 4 + i)

    steps(9, 13, sort_some)

    def group(j):
        span = pl.ds(pl.multiple_of(j * QW, 16), QW)
        for c in range(3):
            acc[c] += jnp.dot(xq[c // 2, j], wbuf[c, span, :], preferred_element_type=F32)

    j, r = w // 8, lax.rem(w, 8)
    near = lax.rem(j + jnp.where(r <= 3, 3, 1), 4)
    far = lax.rem(j + jnp.where(r <= 3, 1, 3), 4)
    group(j)
    steps(13, 14)
    group(near)
    steps(14, 15)
    last = ((0, 0, 0, SH), (1, 2, 0, SH), (0, 1, 0, 64), (1, 1, 64, 48))
    for way, c in TURNS:
        landed(way, HALF - 1, c).wait_recv()
        for way_l, c_l, lo, size in last:
            if (way_l, c_l) == (way, c):
                hop(way, HALF, c, lo, size).start()
    group(far)
    for way, c, lo, size in last:
        landed(way, HALF, c, lo, size).wait_recv()
    group(lax.rem(j + 2, 4))

    gate, up, raw = acc[0], acc[1], acc[2]
    sigma = 1.0 / (1.0 + jnp.exp(-gate))
    act = gate * sigma
    slope = sigma * (1.0 + gate * (1.0 - sigma))
    d_gate = (raw * up * slope).astype(BF16)
    d_up = (raw * act).astype(BF16)
    score = jnp.sum(act * up * raw, axis=1, keepdims=True)

    row = lax.broadcasted_iota(jnp.int32, (ROWS, 128), 0)
    col = lax.broadcasted_iota(jnp.int32, (ROWS, 128), 1)
    slot = lax.rem(row, 4)
    high = score.astype(BF16).astype(F32)
    marks = jnp.where(col == slot, high, 0.0) + jnp.where(col == slot + 8, score - high, 0.0)
    marks = marks + pltpu.roll(marks, 1, 0)
    marks = marks + pltpu.roll(marks, 2, 0)
    marks = jnp.where(slot == 3, marks, 0.0)

    mine = pl.multiple_of(core * 64, 64)
    other = pl.multiple_of((1 - core) * 64, 64)
    gives, tooks, outs, rins = (give_a, give_b), (took_a, took_b), (out_a, out_b), (rin_a, rin_b)

    def c_copy(h):
        return pltpu.make_async_remote_copy(
            src_ref=gives[h],
            dst_ref=tooks[h],
            send_sem=c_send.at[h],
            recv_sem=c_recv.at[h],
            device_id=(w, sibling),
            device_id_type=MESH,
        )

    nt = (((1,), (1,)), ((), ()))
    for h, (lo, size) in enumerate(CUTS):
        for q in range(NQ):
            span = pl.ds(q * QW + lo, size)
            dxs[q, :, lo : lo + size] = lax.dot_general(
                d_gate, wbuf[0, span, :], nt, preferred_element_type=F32
            ) + lax.dot_general(d_up, wbuf[1, span, :], nt, preferred_element_type=F32)
            if q == 0 and h == 0:
                dxs[0, :, 0:128] += marks
            gives[h][q] = dxs[q, pl.ds(other, 64), lo : lo + size].astype(BF16)
        c_copy(h).start()

    def r_copy(h, dest):
        return pltpu.make_async_remote_copy(
            src_ref=outs[h].at[dest],
            dst_ref=rins[h].at[chip],
            send_sem=r_send.at[h * 16 + dest],
            recv_sem=r_recv.at[h * 16 + chip],
            device_id=(w, dest * 2 + core),
            device_id_type=MESH,
        )

    def r_landed(h, origin):
        return pltpu.make_async_remote_copy(
            src_ref=outs[h].at[0],
            dst_ref=rins[h].at[origin],
            send_sem=r_send.at[h * 16 + origin],
            recv_sem=r_recv.at[h * 16 + origin],
            device_id=(w, n),
            device_id_type=MESH,
        )

    own_r = [load(5 + 2 * h, outs[h].at[chip], rins[h].at[chip]) for h in range(2)]
    mark_rows = (lax.broadcasted_iota(jnp.int32, (8, 128), 0) % 4) == 3
    for h, (lo, size) in enumerate(CUTS):
        c_copy(h).wait_recv()
        low = lax.broadcasted_iota(jnp.int32, (8, size), 0) < 4
        for turn in range(4):
            g = lax.rem(my_exp + turn, 4)
            for i in range(2):
                here = pl.ds(pl.multiple_of(mine + g * 16 + i * 8, 8), 8)
                there = pl.ds(pl.multiple_of(g * 16, 16), 16)
                v = [
                    dxs[q, here, lo : lo + size] + tooks[h][q, there, :].astype(F32)[i * 8 : i * 8 + 8]
                    for q in range(NQ)
                ]
                if h == 0:
                    head = v[0][:, 0:128]
                    rest = head - head.astype(BF16).astype(F32)
                    head = head + jnp.where(mark_rows, pltpu.roll(rest, 8, 1), 0.0)
                    v[0] = jnp.concatenate([head, v[0][:, 128:]], 1)
                r = [pltpu.roll(one, 4, 0) for one in v]
                first = [jnp.where(low, v[0], r[1]), jnp.where(low, v[2], r[3])]
                second = [jnp.where(low, r[0], v[1]), jnp.where(low, r[2], v[3])]
                outs[h][4 * g + 2 * i] = jnp.concatenate(first, 0).astype(BF16)
                outs[h][4 * g + 2 * i + 1] = jnp.concatenate(second, 0).astype(BF16)
            for i in range(4):
                dest = 4 * g + lax.rem(chip + i, 4)
                if turn == 0 and i == 0:
                    own_r[h].start()
                else:
                    r_copy(h, dest).start()

    sent(HALF - 2)
    sent(HALF - 1)
    for way, c, lo, size in last:
        hop(way, HALF, c, lo, size).wait_send()
    for h in range(2):
        c_copy(h).wait_send()
        own_r[h].wait()

    def r_wait(d, carry):
        for h in range(2):
            r_landed(h, lax.rem(chip + d, NP // 2)).wait_recv()
        return carry

    lax.fori_loop(1, NP // 2, r_wait, 0)

    def r_done(d, carry):
        for h in range(2):
            r_copy(h, lax.rem(chip + d, NP // 2)).wait_send()
        return carry

    lax.fori_loop(1, NP // 2, r_done, 0)


def combine(rin_a, rin_b, spread_ref, ids_ref, slots_ref, grad_ref, prob_ref):
    spread = spread_ref[...].astype(F32)
    lane_q = lax.rem(lax.broadcasted_iota(jnp.int32, (TOK, LANES), 1) // 4, NQ)
    mixes = [jnp.where(lane_q == q, spread, 0.0).astype(BF16) for q in range(NQ)]
    for ref, (lo, size) in ((rin_a, CUTS[0]), (rin_b, CUTS[1])):
        rows = ref[...].reshape(LANES, size)
        for q in range(NQ):
            grad_ref[:, q * QW + lo : q * QW + lo + size] = jnp.dot(
                mixes[q], rows, preferred_element_type=F32
            ).astype(BF16)
    rows = rin_a[:, :, 0:128].reshape(LANES, 128)

    s_row = lax.broadcasted_iota(jnp.int32, (16, LANES), 0)
    s_col = lax.broadcasted_iota(jnp.int32, (16, LANES), 1)
    take = (lax.rem(s_col, 16) == 3) & (s_col // 64 == s_row)
    sums = jnp.dot(jnp.where(take, 1.0, 0.0).astype(BF16), rows, preferred_element_type=F32)
    target = target_of(ids_ref, slots_ref)
    result = jnp.zeros((8, TOK), F32)
    for e in range(EXP):
        for s in range(3):
            value = sums[e : e + 1, s : s + 1] + sums[e : e + 1, s + 8 : s + 9]
            result = jnp.where(target == e * 4 + s, value, result)
    prob_ref[...] = result


def shards(tokens, cotangent, expert_ids, slots, probs, w_gate, w_up, w_down):
    any_spec = pl.BlockSpec(memory_space=pl.ANY)
    vmem = pl.BlockSpec(memory_space=pltpu.VMEM)
    ring_sems = 2 * (HALF + 1) * 3
    ids_t, slots_t = expert_ids.T, slots.T
    rins_a, rins_b, spread = pl.pallas_call(
        kernel,
        out_shape=(
            jax.ShapeDtypeStruct((NP // 2, 16, CUTS[0][1]), BF16),
            jax.ShapeDtypeStruct((NP // 2, 16, CUTS[1][1]), BF16),
            jax.ShapeDtypeStruct((TOK, LANES), BF16),
        ),
        in_specs=[any_spec, any_spec, vmem, vmem, vmem, any_spec, any_spec, any_spec],
        out_specs=(any_spec, any_spec, vmem),
        scratch_shapes=[
            pltpu.VMEM((3, D, HID), BF16),
            pltpu.VMEM((TOK, D), BF16),
            pltpu.VMEM((TOK, D), BF16),
            pltpu.VMEM((EXP, 2, 16, QW), BF16),
            pltpu.VMEM((2, NP, 16, QW), BF16),
            pltpu.VMEM((2, NQ, ROWS, QW), BF16),
            pltpu.VMEM((3, ROWS, HID), F32),
            pltpu.VMEM((NQ, ROWS, QW), F32),
            pltpu.VMEM((NQ, ROWS // 2, CUTS[0][1]), BF16),
            pltpu.VMEM((NQ, ROWS // 2, CUTS[1][1]), BF16),
            pltpu.VMEM((NQ, ROWS // 2, CUTS[0][1]), BF16),
            pltpu.VMEM((NQ, ROWS // 2, CUTS[1][1]), BF16),
            pltpu.VMEM((NP // 2, 16, CUTS[0][1]), BF16),
            pltpu.VMEM((NP // 2, 16, CUTS[1][1]), BF16),
            pltpu.SemaphoreType.DMA((8,)),
            pltpu.SemaphoreType.DMA((ring_sems,)),
            pltpu.SemaphoreType.DMA((ring_sems,)),
            pltpu.SemaphoreType.DMA((NP,)),
            pltpu.SemaphoreType.DMA((NP,)),
            pltpu.SemaphoreType.DMA((2,)),
            pltpu.SemaphoreType.DMA((2,)),
            pltpu.SemaphoreType.DMA((NP,)),
            pltpu.SemaphoreType.DMA((NP,)),
            pltpu.SemaphoreType.REGULAR((4,)),
        ],
        compiler_params=pltpu.CompilerParams(
            collective_id=0, has_side_effects=True, vmem_limit_bytes=56 * 1024 * 1024
        ),
    )(tokens, cotangent, ids_t, slots_t, probs.T, w_gate, w_up, w_down.T)
    grad, prob_t = pl.pallas_call(
        combine,
        out_shape=(jax.ShapeDtypeStruct((TOK, D), BF16), jax.ShapeDtypeStruct((8, TOK), F32)),
        in_specs=[vmem] * 5,
        out_specs=(vmem, vmem),
    )(rins_a, rins_b, spread, ids_t, slots_t)
    return grad, prob_t.T


def solution(mesh):
    rows = P(("wide", "narrow"), None)
    in_specs = (rows, rows, rows, rows, rows, P("wide", "narrow"), P("wide", "narrow"), P("narrow", "wide"))
    return jax.shard_map(shards, mesh=mesh, in_specs=in_specs, out_specs=(rows, rows), check_vma=False)
```

```python
import functools

import jax
import jax.numpy as jnp
from jax import lax
from jax.experimental import pallas as pl
from jax.experimental.pallas import tpu as pltpu
from jax.sharding import PartitionSpec as P

MESH = pl.DeviceIdType.MESH
F32 = jnp.float32
BF16 = jnp.bfloat16

NZ = 32
NP = 32
EXP = 4
PER_EXP = 8
TOK = 128
D = 3584
HID = 256
SH = 112
NQ = 4
QW = D // NQ
LANES = NP * 8
ROWS = NP * 4
HALF = NZ // 2
FAR_FIRST = (2, 1, 3, 0)
MOST = HALF + 2
CUTS = ((0, 512), (512, 384))


def place(n):
    return lax.rem(n, 2) * (NP // 2) + n // 2


def lean(z):
    return jnp.where(z < 5, 1, 0)


def target_of(ids_ref, slots_ref):
    ids = ids_ref[...]
    return jnp.where(ids < EXP, ids * 4 + slots_ref[...], -1)


def one_hot(target, code, value=None):
    total = jnp.zeros(code.shape, F32)
    for k in range(8):
        held = 1.0 if value is None else value[k : k + 1]
        total = total + jnp.where(target[k : k + 1] == code, held, 0.0)
    return total


def kernel(
    tok_hbm, cot_hbm, ids_hbm, slots_hbm, probs_hbm, wg_hbm, wu_hbm, wd_hbm,
    rin_a, rin_b, spread_hbm,
    ids_ref, slots_ref, probs_ref, spread_ref, wbuf, tok, cot, msg, xin, xq, acc, dxs, give_a, give_b, took_a, took_b, out_a, out_b,
    loc_sem, ring_send, ring_recv, cross_send, cross_recv, x_send, x_recv, c_send, c_recv, r_send, r_recv, word,
):
    w = lax.axis_index("wide")
    n = lax.axis_index("narrow")
    right, left = lax.rem(w + 1, NZ), lax.rem(w + NZ - 1, NZ)
    core, chip = lax.rem(n, 2), n // 2
    my_place = place(n)
    my_exp = n // PER_EXP

    def load(i, src, dst):
        return pltpu.make_async_copy(src, dst, loc_sem.at[i])

    def rows_of(shard):
        return pl.ds(pl.multiple_of(shard * SH, 16), SH)

    loads = [
        load(0, wg_hbm, wbuf.at[core, 0, rows_of(w)]),
        load(1, wu_hbm, wbuf.at[core, 1, rows_of(w)]),
        load(6, wd_hbm, wbuf.at[core, 2, rows_of(w)]),
        load(2, tok_hbm, tok),
        load(3, cot_hbm, cot),
        load(8, ids_hbm, ids_ref),
        load(9, slots_hbm, slots_ref),
        load(10, probs_hbm, probs_ref),
    ]
    for one in loads:
        one.start()

    side = 4 * (chip // 4)
    sibling = chip * 2 + 1 - core
    beside = [(side + lax.rem(chip + d, 4)) * 2 + core for d in (1, 3)]
    above = [lax.rem(chip + d, NP // 2) * 2 + core for d in (4, 12)]
    barrier = pltpu.get_barrier_semaphore()
    for to in [(z, chip * 2 + i) for z in (left, right) for i in (0, 1)] + [(w, sibling)] + [(w, one) for one in beside + above]:
        pl.semaphore_signal(barrier, inc=1, device_id=to, device_id_type=MESH)
    pl.semaphore_wait(barrier, 9)

    def tell(i, whom):
        for one in whom:
            pl.semaphore_signal(word.at[i], inc=1, device_id=(w, one), device_id_type=MESH)

    def hear(i, whom):
        pl.semaphore_wait(word.at[i], len(whom))

    tell(0, beside)

    onward = jnp.where(core == 0, right, left)
    reach = jnp.where(core == 0, HALF - 1 - lean(w), HALF - 1 + lean(w))
    reach_next = jnp.where(core == 0, HALF - 1 - lean(onward), HALF - 1 + lean(onward))
    reach_other = jnp.where(core == 0, HALF - 1 + lean(w), HALF - 1 - lean(w))
    extra = (1, 1 - core, 0)
    extra_other = (1, core, 0)

    def weight(j, way):
        return j + way * (2 - 2 * j)

    def shard_at(k, way):
        return jnp.where(way == 0, lax.rem(w + NZ - k, NZ), lax.rem(w + k, NZ))

    def sem_at(k, o, j):
        return (k * 2 + o) * 3 + j

    def first_hop(way, c):
        j = weight(c, way)
        return pltpu.make_async_remote_copy(
            src_ref=(wg_hbm, wu_hbm, wd_hbm)[c],
            dst_ref=wbuf.at[core, c, rows_of(w)],
            send_sem=ring_send.at[sem_at(0, way, j)],
            recv_sem=ring_recv.at[sem_at(1, core, j)],
            device_id=((right, left)[way], chip * 2 + way),
            device_id_type=MESH,
        )

    def hop(k, o, j):
        here = wbuf.at[o, weight(j, core), rows_of(shard_at(k, core))]
        return pltpu.make_async_remote_copy(
            src_ref=here,
            dst_ref=here,
            send_sem=ring_send.at[sem_at(k, o, j)],
            recv_sem=ring_recv.at[sem_at(k + 1, o, j)],
            device_id=(onward, n),
            device_id_type=MESH,
        )

    def landed(k, o, j):
        here = wbuf.at[o, weight(j, core), rows_of(shard_at(k, core))]
        return pltpu.make_async_remote_copy(
            src_ref=here,
            dst_ref=here,
            send_sem=ring_send.at[sem_at(k, o, j)],
            recv_sem=ring_recv.at[sem_at(k, o, j)],
            device_id=(onward, n),
            device_id_type=MESH,
        )

    def cross(k, j, owner, way):
        here = wbuf.at[owner, weight(j, way), rows_of(shard_at(k, way))]
        return pltpu.make_async_remote_copy(
            src_ref=here,
            dst_ref=here,
            send_sem=cross_send.at[k * 3 + j],
            recv_sem=cross_recv.at[k * 3 + j],
            device_id=(w, sibling),
            device_id_type=MESH,
        )

    for i in range(3):
        for way in (0, 1):
            first_hop(way, weight(i, way)).start()

    def step(k):
        for j in range(3):

            @pl.when(k <= reach + extra[j])
            def _():
                for o in range(2):
                    landed(k, o, j).wait_recv()

                    @pl.when(k < reach_next + extra[j])
                    def _():
                        hop(k, o, j).start()

                cross(k, j, 1 - core, core).start()

    def sent(k):
        for j in range(3):

            @pl.when(k < reach_next + extra[j])
            def _():
                for o in range(2):
                    hop(k, o, j).wait_send()

            @pl.when(k <= reach + extra[j])
            def _():
                cross(k, j, 1 - core, core).wait_send()

    def crossed(k):
        for j in range(3):

            @pl.when(k <= reach_other + extra_other[j])
            def _():
                cross(k, j, core, 1 - core).wait_recv()

    def steps(lo, hi, more=None):
        def body(k, carry):
            step(k)
            if lo >= 3:
                sent(k - 2)
            if lo >= 8:
                crossed(k - 7)
            if more is not None:
                more(k)
            return carry

        lax.fori_loop(lo, hi, body, 0)

    for one in loads[5:]:
        one.wait()
    target = target_of(ids_ref, slots_ref)
    row = lax.broadcasted_iota(jnp.int32, (64, TOK), 0)
    picks = one_hot(target, (row // 16) * 4 + lax.rem(row, 4)).astype(BF16)
    row_q = lax.rem(lax.broadcasted_iota(jnp.int32, (64, QW), 0) // 4, NQ)

    def pick_rows(a, src):
        rows = jnp.zeros((64, QW), F32)
        for q in range(NQ):
            part = jnp.dot(picks, src[:, q * QW : (q + 1) * QW], preferred_element_type=F32)
            rows = jnp.where(row_q == q, part, rows)
        for e in range(EXP):
            msg[e, a] = rows[e * 16 : (e + 1) * 16].astype(BF16)

    def x_copy(d):
        dest = lax.rem(n + d, NP)
        return pltpu.make_async_remote_copy(
            src_ref=msg.at[dest // PER_EXP],
            dst_ref=xin.at[:, my_place],
            send_sem=x_send.at[d],
            recv_sem=x_recv.at[my_place],
            device_id=(w, dest),
            device_id_type=MESH,
        )

    def x_landed(d):
        origin = place(lax.rem(n + d, NP))
        return pltpu.make_async_remote_copy(
            src_ref=msg.at[0],
            dst_ref=xin.at[:, origin],
            send_sem=x_send.at[d],
            recv_sem=x_recv.at[origin],
            device_id=(w, n),
            device_id_type=MESH,
        )

    def x_start(d, carry):
        x_copy(d).start()
        return carry

    loads[3].wait()
    pick_rows(0, tok)
    hear(0, beside)
    tell(1, beside)
    loads[4].wait()
    pick_rows(1, cot)
    hear(1, beside)
    tell(2, above)
    acc[...] = jnp.zeros_like(acc)
    hear(2, above)
    tell(3, [sibling])
    steps(1, 2)
    hear(3, [sibling])
    lax.fori_loop(1, NP, x_start, 0)
    own_x = load(4, msg.at[my_exp], xin.at[:, my_place])
    own_x.start()
    steps(2, 3)
    row = lax.broadcasted_iota(jnp.int32, (LANES, TOK), 0)
    spread_ref[...] = jnp.transpose(
        one_hot(target, (row // 64) * 4 + lax.rem(row, 4), probs_ref[...].astype(F32))
    ).astype(BF16)
    save = load(11, spread_ref, spread_hbm)
    save.start()
    own_x.wait()
    for one in loads[:3]:
        one.wait()
    steps(3, 8)
    steps(8, 12)

    def x_done(d, carry):
        x_copy(d).wait_send()
        return carry

    lax.fori_loop(1, NP, x_done, 0)

    def x_wait(d, carry):
        x_landed(d).wait_recv()
        return carry

    lax.fori_loop(1, NP, x_wait, 0)

    low = lax.broadcasted_iota(jnp.int32, (8, QW), 0) < 4

    def sort_rows(unit):
        a, g = unit // 8, lax.rem(unit, 8)
        block = [xin[a, 4 * g + i].astype(F32) for i in range(4)]
        for half in range(2):
            v = [one[half * 8 : half * 8 + 8] for one in block]
            r = [pltpu.roll(one, 4, 0) for one in v]
            even = [jnp.where(low, v[0], r[1]), jnp.where(low, v[2], r[3])]
            odd = [jnp.where(low, r[0], v[1]), jnp.where(low, r[2], v[3])]
            span = pl.ds(pl.multiple_of(g * 16, 16), 16)
            xq[a, 2 * half, span, :] = jnp.concatenate(even, 0).astype(BF16)
            xq[a, 2 * half + 1, span, :] = jnp.concatenate(odd, 0).astype(BF16)

    def sort_some(k):
        for i in range(4):
            sort_rows((k - 12) * 4 + i)

    save.wait()
    steps(12, 16, sort_some)

    def group(j):
        span = pl.ds(pl.multiple_of(j * QW, 16), QW)
        for c in range(3):
            acc[c] += jnp.dot(xq[c // 2, j], wbuf[core, c, span, :], preferred_element_type=F32)

    j, r = w // 8, lax.rem(w, 8)
    near = lax.rem(j + jnp.where(r <= 3, 3, 1), 4)
    far = lax.rem(j + jnp.where(r <= 3, 1, 3), 4)
    group(j)
    steps(16, MOST + 1)
    group(near)
    for k in range(MOST - 6, HALF):
        crossed(k)
    group(far)
    for k in range(HALF, MOST + 1):
        crossed(k)
    group(lax.rem(j + 2, 4))

    gate, up, raw = acc[0], acc[1], acc[2]
    sigma = 1.0 / (1.0 + jnp.exp(-gate))
    act = gate * sigma
    slope = sigma * (1.0 + gate * (1.0 - sigma))
    d_gate = (raw * up * slope).astype(BF16)
    d_up = (raw * act).astype(BF16)
    score = jnp.sum(act * up * raw, axis=1, keepdims=True)

    row = lax.broadcasted_iota(jnp.int32, (ROWS, 128), 0)
    col = lax.broadcasted_iota(jnp.int32, (ROWS, 128), 1)
    slot = lax.rem(row, 4)
    high = score.astype(BF16).astype(F32)
    marks = jnp.where(col == slot, high, 0.0) + jnp.where(col == slot + 8, score - high, 0.0)
    marks = marks + pltpu.roll(marks, 1, 0)
    marks = marks + pltpu.roll(marks, 2, 0)
    marks = jnp.where(slot == 3, marks, 0.0)

    mine = pl.multiple_of(core * 64, 64)
    other = pl.multiple_of((1 - core) * 64, 64)
    gives, tooks, outs, rins = (give_a, give_b), (took_a, took_b), (out_a, out_b), (rin_a, rin_b)

    def c_copy(h):
        return pltpu.make_async_remote_copy(
            src_ref=gives[h],
            dst_ref=tooks[h],
            send_sem=c_send.at[h],
            recv_sem=c_recv.at[h],
            device_id=(w, sibling),
            device_id_type=MESH,
        )

    nt = (((1,), (1,)), ((), ()))
    for h, (lo, size) in enumerate(CUTS):
        for q in range(NQ):
            span = pl.ds(q * QW + lo, size)
            dxs[q, :, lo : lo + size] = lax.dot_general(
                d_gate, wbuf[core, 0, span, :], nt, preferred_element_type=F32
            ) + lax.dot_general(d_up, wbuf[core, 1, span, :], nt, preferred_element_type=F32)
            if q == 0 and h == 0:
                dxs[0, :, 0:128] += marks
            gives[h][q] = dxs[q, pl.ds(other, 64), lo : lo + size].astype(BF16)
        c_copy(h).start()

    def r_copy(h, dest):
        return pltpu.make_async_remote_copy(
            src_ref=outs[h].at[dest],
            dst_ref=rins[h].at[chip],
            send_sem=r_send.at[h * 16 + dest],
            recv_sem=r_recv.at[h * 16 + chip],
            device_id=(w, dest * 2 + core),
            device_id_type=MESH,
        )

    def r_landed(h, origin):
        return pltpu.make_async_remote_copy(
            src_ref=outs[h].at[0],
            dst_ref=rins[h].at[origin],
            send_sem=r_send.at[h * 16 + origin],
            recv_sem=r_recv.at[h * 16 + origin],
            device_id=(w, n),
            device_id_type=MESH,
        )

    own_r = [load(5 + 2 * h, outs[h].at[chip], rins[h].at[chip]) for h in range(2)]
    mark_rows = (lax.broadcasted_iota(jnp.int32, (8, 128), 0) % 4) == 3
    for h, (lo, size) in enumerate(CUTS):
        c_copy(h).wait_recv()
        low = lax.broadcasted_iota(jnp.int32, (8, size), 0) < 4
        for turn in FAR_FIRST:
            g = lax.rem(my_exp + turn, 4)
            for i in range(2):
                here = pl.ds(pl.multiple_of(mine + g * 16 + i * 8, 8), 8)
                there = pl.ds(pl.multiple_of(g * 16, 16), 16)
                v = [
                    dxs[q, here, lo : lo + size] + tooks[h][q, there, :].astype(F32)[i * 8 : i * 8 + 8]
                    for q in range(NQ)
                ]
                if h == 0:
                    head = v[0][:, 0:128]
                    rest = head - head.astype(BF16).astype(F32)
                    head = head + jnp.where(mark_rows, pltpu.roll(rest, 8, 1), 0.0)
                    v[0] = jnp.concatenate([head, v[0][:, 128:]], 1)
                r = [pltpu.roll(one, 4, 0) for one in v]
                first = [jnp.where(low, v[0], r[1]), jnp.where(low, v[2], r[3])]
                second = [jnp.where(low, r[0], v[1]), jnp.where(low, r[2], v[3])]
                outs[h][4 * g + 2 * i] = jnp.concatenate(first, 0).astype(BF16)
                outs[h][4 * g + 2 * i + 1] = jnp.concatenate(second, 0).astype(BF16)
            for i in FAR_FIRST:
                dest = 4 * g + lax.rem(chip + i, 4)
                if turn == 0 and i == 0:
                    own_r[h].start()
                else:
                    r_copy(h, dest).start()

    for way in (0, 1):
        for c in range(3):
            first_hop(way, c).wait_send()
    for k in (MOST - 1, MOST):
        sent(k)
    for h in range(2):
        c_copy(h).wait_send()
        own_r[h].wait()

    def r_done(d, carry):
        for h in range(2):
            r_copy(h, lax.rem(chip + d, NP // 2)).wait_send()
        return carry

    lax.fori_loop(1, NP // 2, r_done, 0)

    def r_wait(d, carry):
        for h in range(2):
            r_landed(h, lax.rem(chip + d, NP // 2)).wait_recv()
        return carry

    lax.fori_loop(1, NP // 2, r_wait, 0)


def combine(rin_a, rin_b, spread_ref, ids_ref, slots_ref, grad_ref, prob_ref):
    spread = spread_ref[...].astype(F32)
    lane_q = lax.rem(lax.broadcasted_iota(jnp.int32, (TOK, LANES), 1) // 4, NQ)
    mixes = [jnp.where(lane_q == q, spread, 0.0).astype(BF16) for q in range(NQ)]
    for ref, (lo, size) in ((rin_a, CUTS[0]), (rin_b, CUTS[1])):
        rows = ref[...].reshape(LANES, size)
        for q in range(NQ):
            grad_ref[:, q * QW + lo : q * QW + lo + size] = jnp.dot(
                mixes[q], rows, preferred_element_type=F32
            ).astype(BF16)
    rows = rin_a[:, :, 0:128].reshape(LANES, 128)

    s_row = lax.broadcasted_iota(jnp.int32, (16, LANES), 0)
    s_col = lax.broadcasted_iota(jnp.int32, (16, LANES), 1)
    take = (lax.rem(s_col, 16) == 3) & (s_col // 64 == s_row)
    sums = jnp.dot(jnp.where(take, 1.0, 0.0).astype(BF16), rows, preferred_element_type=F32)
    target = target_of(ids_ref, slots_ref)
    result = jnp.zeros((8, TOK), F32)
    for e in range(EXP):
        for s in range(3):
            value = sums[e : e + 1, s : s + 1] + sums[e : e + 1, s + 8 : s + 9]
            result = jnp.where(target == e * 4 + s, value, result)
    prob_ref[...] = result


def shards(tokens, cotangent, expert_ids, slots, probs, w_gate, w_up, w_down):
    any_spec = pl.BlockSpec(memory_space=pl.ANY)
    vmem = pl.BlockSpec(memory_space=pltpu.VMEM)
    ring_sems = (MOST + 2) * 6
    ids_t, slots_t = expert_ids.T, slots.T
    rins_a, rins_b, spread = pl.pallas_call(
        kernel,
        out_shape=(
            jax.ShapeDtypeStruct((NP // 2, 16, CUTS[0][1]), BF16),
            jax.ShapeDtypeStruct((NP // 2, 16, CUTS[1][1]), BF16),
            jax.ShapeDtypeStruct((TOK, LANES), BF16),
        ),
        in_specs=[any_spec] * 8,
        out_specs=(any_spec, any_spec, any_spec),
        scratch_shapes=[
            pltpu.VMEM((8, TOK), jnp.int32),
            pltpu.VMEM((8, TOK), jnp.int32),
            pltpu.VMEM((8, TOK), BF16),
            pltpu.VMEM((TOK, LANES), BF16),
            pltpu.VMEM((2, 3, D, HID), BF16),
            pltpu.VMEM((TOK, D), BF16),
            pltpu.VMEM((TOK, D), BF16),
            pltpu.VMEM((EXP, 2, 16, QW), BF16),
            pltpu.VMEM((2, NP, 16, QW), BF16),
            pltpu.VMEM((2, NQ, ROWS, QW), BF16),
            pltpu.VMEM((3, ROWS, HID), F32),
            pltpu.VMEM((NQ, ROWS, QW), F32),
            pltpu.VMEM((NQ, ROWS // 2, CUTS[0][1]), BF16),
            pltpu.VMEM((NQ, ROWS // 2, CUTS[1][1]), BF16),
            pltpu.VMEM((NQ, ROWS // 2, CUTS[0][1]), BF16),
            pltpu.VMEM((NQ, ROWS // 2, CUTS[1][1]), BF16),
            pltpu.VMEM((NP // 2, 16, CUTS[0][1]), BF16),
            pltpu.VMEM((NP // 2, 16, CUTS[1][1]), BF16),
            pltpu.SemaphoreType.DMA((12,)),
            pltpu.SemaphoreType.DMA((ring_sems,)),
            pltpu.SemaphoreType.DMA((ring_sems,)),
            pltpu.SemaphoreType.DMA((ring_sems // 2,)),
            pltpu.SemaphoreType.DMA((ring_sems // 2,)),
            pltpu.SemaphoreType.DMA((NP,)),
            pltpu.SemaphoreType.DMA((NP,)),
            pltpu.SemaphoreType.DMA((2,)),
            pltpu.SemaphoreType.DMA((2,)),
            pltpu.SemaphoreType.DMA((NP,)),
            pltpu.SemaphoreType.DMA((NP,)),
            pltpu.SemaphoreType.REGULAR((4,)),
        ],
        compiler_params=pltpu.CompilerParams(
            collective_id=0, has_side_effects=True, vmem_limit_bytes=56 * 1024 * 1024
        ),
    )(tokens, cotangent, ids_t, slots_t, probs.T, w_gate, w_up, w_down.T)
    grad, prob_t = pl.pallas_call(
        combine,
        out_shape=(jax.ShapeDtypeStruct((TOK, D), BF16), jax.ShapeDtypeStruct((8, TOK), F32)),
        in_specs=[vmem] * 5,
        out_specs=(vmem, vmem),
    )(rins_a, rins_b, spread, ids_t, slots_t)
    return grad, prob_t.T


def solution(mesh):
    rows = P(("wide", "narrow"), None)
    in_specs = (rows, rows, rows, rows, rows, P("wide", "narrow"), P("wide", "narrow"), P("narrow", "wide"))
    return jax.shard_map(shards, mesh=mesh, in_specs=in_specs, out_specs=(rows, rows), check_vma=False)
```

```python
import functools

import jax
import jax.numpy as jnp
from jax import lax
from jax.experimental import pallas as pl
from jax.experimental.pallas import tpu as pltpu
from jax.sharding import PartitionSpec as P

MESH = pl.DeviceIdType.MESH
F32 = jnp.float32
BF16 = jnp.bfloat16

NZ = 32
NP = 32
EXP = 4
PER_EXP = 8
TOK = 128
D = 3584
HID = 256
SH = 112
NQ = 4
QW = D // NQ
LANES = NP * 8
ROWS = NP * 4
HALF = NZ // 2
FAR_FIRST = (2, 1, 3, 0)
MOST = HALF + 2
CUTS = ((0, 512), (512, 384))


def place(n):
    return lax.rem(n, 2) * (NP // 2) + n // 2


def lean(z):
    return jnp.where(z < 5, 1, 0)


def target_of(ids_ref, slots_ref):
    ids = ids_ref[...]
    return jnp.where(ids < EXP, ids * 4 + slots_ref[...], -1)


def one_hot(target, code, value=None):
    total = jnp.zeros(code.shape, F32)
    for k in range(8):
        held = 1.0 if value is None else value[k : k + 1]
        total = total + jnp.where(target[k : k + 1] == code, held, 0.0)
    return total


def kernel(
    tok_hbm, cot_hbm, ids_hbm, slots_hbm, probs_hbm, wg_hbm, wu_hbm, wd_hbm,
    rin_a, rin_b, spread_hbm,
    ids_ref, slots_ref, probs_ref, spread_ref, wbuf, tok, cot, msg, xin, xq, acc, dxs, give_a, give_b, took_a, took_b, out_a, out_b,
    loc_sem, ring_send, ring_recv, cross_send, cross_recv, x_send, x_recv, c_send, c_recv, r_send, r_recv, word,
):
    w = lax.axis_index("wide")
    n = lax.axis_index("narrow")
    right, left = lax.rem(w + 1, NZ), lax.rem(w + NZ - 1, NZ)
    core, chip = lax.rem(n, 2), n // 2
    my_place = place(n)
    my_exp = n // PER_EXP

    def load(i, src, dst):
        return pltpu.make_async_copy(src, dst, loc_sem.at[i])

    def rows_of(shard):
        return pl.ds(pl.multiple_of(shard * SH, 16), SH)

    loads = [
        load(0, wg_hbm, wbuf.at[core, 0, rows_of(w)]),
        load(1, wu_hbm, wbuf.at[core, 1, rows_of(w)]),
        load(6, wd_hbm, wbuf.at[core, 2, rows_of(w)]),
        load(2, tok_hbm, tok),
        load(3, cot_hbm, cot),
        load(8, ids_hbm, ids_ref),
        load(9, slots_hbm, slots_ref),
        load(10, probs_hbm, probs_ref),
    ]
    for one in loads:
        one.start()

    side = 4 * (chip // 4)
    sibling = chip * 2 + 1 - core
    beside = [(side + lax.rem(chip + d, 4)) * 2 + core for d in (1, 3)]
    above = [lax.rem(chip + d, NP // 2) * 2 + core for d in (4, 12)]
    barrier = pltpu.get_barrier_semaphore()
    for to in [(z, chip * 2 + i) for z in (left, right) for i in (0, 1)] + [(w, sibling)] + [(w, one) for one in beside + above]:
        pl.semaphore_signal(barrier, inc=1, device_id=to, device_id_type=MESH)
    pl.semaphore_wait(barrier, 9)

    def tell(i, whom):
        for one in whom:
            pl.semaphore_signal(word.at[i], inc=1, device_id=(w, one), device_id_type=MESH)

    def hear(i, whom):
        pl.semaphore_wait(word.at[i], len(whom))

    tell(0, beside)

    onward = jnp.where(core == 0, right, left)
    reach = jnp.where(core == 0, HALF - 1 - lean(w), HALF - 1 + lean(w))
    reach_next = jnp.where(core == 0, HALF - 1 - lean(onward), HALF - 1 + lean(onward))
    reach_other = jnp.where(core == 0, HALF - 1 + lean(w), HALF - 1 - lean(w))
    extra = (1, 1 - core, 0)
    extra_other = (1, core, 0)

    def weight(j, way):
        return j + way * (2 - 2 * j)

    def shard_at(k, way):
        return jnp.where(way == 0, lax.rem(w + NZ - k, NZ), lax.rem(w + k, NZ))

    def sem_at(k, o, j):
        return (k * 2 + o) * 3 + j

    def first_hop(way, c):
        j = weight(c, way)
        return pltpu.make_async_remote_copy(
            src_ref=(wg_hbm, wu_hbm, wd_hbm)[c],
            dst_ref=wbuf.at[core, c, rows_of(w)],
            send_sem=ring_send.at[sem_at(0, way, j)],
            recv_sem=ring_recv.at[sem_at(1, core, j)],
            device_id=((right, left)[way], chip * 2 + way),
            device_id_type=MESH,
        )

    def hop(k, o, j):
        here = wbuf.at[o, weight(j, core), rows_of(shard_at(k, core))]
        return pltpu.make_async_remote_copy(
            src_ref=here,
            dst_ref=here,
            send_sem=ring_send.at[sem_at(k, o, j)],
            recv_sem=ring_recv.at[sem_at(k + 1, o, j)],
            device_id=(onward, n),
            device_id_type=MESH,
        )

    def landed(k, o, j):
        here = wbuf.at[o, weight(j, core), rows_of(shard_at(k, core))]
        return pltpu.make_async_remote_copy(
            src_ref=here,
            dst_ref=here,
            send_sem=ring_send.at[sem_at(k, o, j)],
            recv_sem=ring_recv.at[sem_at(k, o, j)],
            device_id=(onward, n),
            device_id_type=MESH,
        )

    def cross(k, j, owner, way):
        here = wbuf.at[owner, weight(j, way), rows_of(shard_at(k, way))]
        return pltpu.make_async_remote_copy(
            src_ref=here,
            dst_ref=here,
            send_sem=cross_send.at[k * 3 + j],
            recv_sem=cross_recv.at[k * 3 + j],
            device_id=(w, sibling),
            device_id_type=MESH,
        )

    for i in range(3):
        for way in (0, 1):
            first_hop(way, weight(i, way)).start()

    def step(k):
        for j in range(3):

            @pl.when(k <= reach + extra[j])
            def _():
                for o in range(2):
                    landed(k, o, j).wait_recv()

                    @pl.when(k < reach_next + extra[j])
                    def _():
                        hop(k, o, j).start()

                cross(k, j, 1 - core, core).start()

    def sent(k):
        for j in range(3):

            @pl.when(k < reach_next + extra[j])
            def _():
                for o in range(2):
                    hop(k, o, j).wait_send()

            @pl.when(k <= reach + extra[j])
            def _():
                cross(k, j, 1 - core, core).wait_send()

    def crossed(k):
        for j in range(3):

            @pl.when(k <= reach_other + extra_other[j])
            def _():
                cross(k, j, core, 1 - core).wait_recv()

    def steps(lo, hi, more=None):
        def body(k, carry):
            step(k)
            if lo >= 3:
                sent(k - 2)
            if 8 <= lo < 12:
                crossed(k - 7)
            if more is not None:
                more(k)
            return carry

        lax.fori_loop(lo, hi, body, 0)

    for one in loads[5:]:
        one.wait()
    target = target_of(ids_ref, slots_ref)
    row = lax.broadcasted_iota(jnp.int32, (64, TOK), 0)
    picks = one_hot(target, (row // 16) * 4 + lax.rem(row, 4)).astype(BF16)
    row_q = lax.rem(lax.broadcasted_iota(jnp.int32, (64, QW), 0) // 4, NQ)

    def pick_rows(a, src):
        rows = jnp.zeros((64, QW), F32)
        for q in range(NQ):
            part = jnp.dot(picks, src[:, q * QW : (q + 1) * QW], preferred_element_type=F32)
            rows = jnp.where(row_q == q, part, rows)
        for e in range(EXP):
            msg[e, a] = rows[e * 16 : (e + 1) * 16].astype(BF16)

    def x_copy(d):
        dest = lax.rem(n + d, NP)
        return pltpu.make_async_remote_copy(
            src_ref=msg.at[dest // PER_EXP],
            dst_ref=xin.at[:, my_place],
            send_sem=x_send.at[d],
            recv_sem=x_recv.at[my_place],
            device_id=(w, dest),
            device_id_type=MESH,
        )

    def x_landed(d):
        origin = place(lax.rem(n + d, NP))
        return pltpu.make_async_remote_copy(
            src_ref=msg.at[0],
            dst_ref=xin.at[:, origin],
            send_sem=x_send.at[d],
            recv_sem=x_recv.at[origin],
            device_id=(w, n),
            device_id_type=MESH,
        )

    def x_start(d, carry):
        x_copy(d).start()
        return carry

    loads[3].wait()
    pick_rows(0, tok)
    hear(0, beside)
    tell(1, beside)
    loads[4].wait()
    pick_rows(1, cot)
    hear(1, beside)
    tell(2, above)
    acc[...] = jnp.zeros_like(acc)
    hear(2, above)
    tell(3, [sibling])
    hear(3, [sibling])
    lax.fori_loop(1, 11, x_start, 0)
    steps(1, 2)
    lax.fori_loop(11, 21, x_start, 0)
    steps(2, 3)
    lax.fori_loop(21, NP, x_start, 0)
    own_x = load(4, msg.at[my_exp], xin.at[:, my_place])
    own_x.start()
    row = lax.broadcasted_iota(jnp.int32, (LANES, TOK), 0)
    spread_ref[...] = jnp.transpose(
        one_hot(target, (row // 64) * 4 + lax.rem(row, 4), probs_ref[...].astype(F32))
    ).astype(BF16)
    save = load(11, spread_ref, spread_hbm)
    save.start()
    own_x.wait()
    for one in loads[:3]:
        one.wait()
    steps(3, 8)
    steps(8, 10)

    def x_done(d, carry):
        x_copy(d).wait_send()
        return carry

    lax.fori_loop(1, NP, x_done, 0)

    def x_wait(d, carry):
        x_landed(d).wait_recv()
        return carry

    lax.fori_loop(1, NP, x_wait, 0)

    low = lax.broadcasted_iota(jnp.int32, (8, QW), 0) < 4

    def sort_rows(unit):
        a, g = unit // 8, lax.rem(unit, 8)
        block = [xin[a, 4 * g + i].astype(F32) for i in range(4)]
        for half in range(2):
            v = [one[half * 8 : half * 8 + 8] for one in block]
            r = [pltpu.roll(one, 4, 0) for one in v]
            even = [jnp.where(low, v[0], r[1]), jnp.where(low, v[2], r[3])]
            odd = [jnp.where(low, r[0], v[1]), jnp.where(low, r[2], v[3])]
            span = pl.ds(pl.multiple_of(g * 16, 16), 16)
            xq[a, 2 * half, span, :] = jnp.concatenate(even, 0).astype(BF16)
            xq[a, 2 * half + 1, span, :] = jnp.concatenate(odd, 0).astype(BF16)

    def sort_some(k):
        for i in range(4):
            sort_rows((k - 10) * 4 + i)

    def hear_some(k):
        for i in range(2):
            crossed(5 + (k - 12) * 2 + i)

    save.wait()
    steps(10, 12, sort_some)
    steps(12, 14, lambda k: (sort_some(k), hear_some(k)))
    crossed(9)

    def group(j):
        span = pl.ds(pl.multiple_of(j * QW, 16), QW)
        for c in range(3):
            acc[c] += jnp.dot(xq[c // 2, j], wbuf[core, c, span, :], preferred_element_type=F32)

    j, r = w // 8, lax.rem(w, 8)
    near = lax.rem(j + jnp.where(r <= 3, 3, 1), 4)
    far = lax.rem(j + jnp.where(r <= 3, 1, 3), 4)
    group(j)
    steps(14, 15)
    crossed(10)
    crossed(11)
    group(near)
    steps(15, MOST + 1)
    for k in range(12, HALF):
        crossed(k)
    group(far)
    for k in range(HALF, MOST + 1):
        crossed(k)
    group(lax.rem(j + 2, 4))

    gate, up, raw = acc[0], acc[1], acc[2]
    sigma = 1.0 / (1.0 + jnp.exp(-gate))
    act = gate * sigma
    slope = sigma * (1.0 + gate * (1.0 - sigma))
    d_gate = (raw * up * slope).astype(BF16)
    d_up = (raw * act).astype(BF16)
    score = jnp.sum(act * up * raw, axis=1, keepdims=True)

    row = lax.broadcasted_iota(jnp.int32, (ROWS, 128), 0)
    col = lax.broadcasted_iota(jnp.int32, (ROWS, 128), 1)
    slot = lax.rem(row, 4)
    high = score.astype(BF16).astype(F32)
    marks = jnp.where(col == slot, high, 0.0) + jnp.where(col == slot + 8, score - high, 0.0)
    marks = marks + pltpu.roll(marks, 1, 0)
    marks = marks + pltpu.roll(marks, 2, 0)
    marks = jnp.where(slot == 3, marks, 0.0)

    mine = pl.multiple_of(core * 64, 64)
    other = pl.multiple_of((1 - core) * 64, 64)
    gives, tooks, outs, rins = (give_a, give_b), (took_a, took_b), (out_a, out_b), (rin_a, rin_b)

    def c_copy(h):
        return pltpu.make_async_remote_copy(
            src_ref=gives[h],
            dst_ref=tooks[h],
            send_sem=c_send.at[h],
            recv_sem=c_recv.at[h],
            device_id=(w, sibling),
            device_id_type=MESH,
        )

    nt = (((1,), (1,)), ((), ()))
    for h, (lo, size) in enumerate(CUTS):
        for q in range(NQ):
            span = pl.ds(q * QW + lo, size)
            dxs[q, :, lo : lo + size] = lax.dot_general(
                d_gate, wbuf[core, 0, span, :], nt, preferred_element_type=F32
            ) + lax.dot_general(d_up, wbuf[core, 1, span, :], nt, preferred_element_type=F32)
            if q == 0 and h == 0:
                dxs[0, :, 0:128] += marks
            gives[h][q] = dxs[q, pl.ds(other, 64), lo : lo + size].astype(BF16)
        c_copy(h).start()

    def r_copy(h, dest):
        return pltpu.make_async_remote_copy(
            src_ref=outs[h].at[dest],
            dst_ref=rins[h].at[chip],
            send_sem=r_send.at[h * 16 + dest],
            recv_sem=r_recv.at[h * 16 + chip],
            device_id=(w, dest * 2 + core),
            device_id_type=MESH,
        )

    def r_landed(h, origin):
        return pltpu.make_async_remote_copy(
            src_ref=outs[h].at[0],
            dst_ref=rins[h].at[origin],
            send_sem=r_send.at[h * 16 + origin],
            recv_sem=r_recv.at[h * 16 + origin],
            device_id=(w, n),
            device_id_type=MESH,
        )

    own_r = [load(5 + 2 * h, outs[h].at[chip], rins[h].at[chip]) for h in range(2)]
    mark_rows = (lax.broadcasted_iota(jnp.int32, (8, 128), 0) % 4) == 3
    for h, (lo, size) in enumerate(CUTS):
        c_copy(h).wait_recv()
        low = lax.broadcasted_iota(jnp.int32, (8, size), 0) < 4
        for turn in FAR_FIRST:
            g = lax.rem(my_exp + turn, 4)
            for i in range(2):
                here = pl.ds(pl.multiple_of(mine + g * 16 + i * 8, 8), 8)
                there = pl.ds(pl.multiple_of(g * 16, 16), 16)
                v = [
                    dxs[q, here, lo : lo + size] + tooks[h][q, there, :].astype(F32)[i * 8 : i * 8 + 8]
                    for q in range(NQ)
                ]
                if h == 0:
                    head = v[0][:, 0:128]
                    rest = head - head.astype(BF16).astype(F32)
                    head = head + jnp.where(mark_rows, pltpu.roll(rest, 8, 1), 0.0)
                    v[0] = jnp.concatenate([head, v[0][:, 128:]], 1)
                r = [pltpu.roll(one, 4, 0) for one in v]
                first = [jnp.where(low, v[0], r[1]), jnp.where(low, v[2], r[3])]
                second = [jnp.where(low, r[0], v[1]), jnp.where(low, r[2], v[3])]
                outs[h][4 * g + 2 * i] = jnp.concatenate(first, 0).astype(BF16)
                outs[h][4 * g + 2 * i + 1] = jnp.concatenate(second, 0).astype(BF16)
            for i in FAR_FIRST:
                dest = 4 * g + lax.rem(chip + i, 4)
                if turn == 0 and i == 0:
                    own_r[h].start()
                else:
                    r_copy(h, dest).start()

    for way in (0, 1):
        for c in range(3):
            first_hop(way, c).wait_send()
    for k in (MOST - 1, MOST):
        sent(k)
    for h in range(2):
        c_copy(h).wait_send()
        own_r[h].wait()

    def r_done(d, carry):
        for h in range(2):
            r_copy(h, lax.rem(chip + d, NP // 2)).wait_send()
        return carry

    lax.fori_loop(1, NP // 2, r_done, 0)

    def r_wait(d, carry):
        for h in range(2):
            r_landed(h, lax.rem(chip + d, NP // 2)).wait_recv()
        return carry

    lax.fori_loop(1, NP // 2, r_wait, 0)


def combine(rin_a, rin_b, spread_ref, ids_ref, slots_ref, grad_ref, prob_ref):
    spread = spread_ref[...].astype(F32)
    lane_q = lax.rem(lax.broadcasted_iota(jnp.int32, (TOK, LANES), 1) // 4, NQ)
    mixes = [jnp.where(lane_q == q, spread, 0.0).astype(BF16) for q in range(NQ)]
    for ref, (lo, size) in ((rin_a, CUTS[0]), (rin_b, CUTS[1])):
        rows = ref[...].reshape(LANES, size)
        for q in range(NQ):
            grad_ref[:, q * QW + lo : q * QW + lo + size] = jnp.dot(
                mixes[q], rows, preferred_element_type=F32
            ).astype(BF16)
    rows = rin_a[:, :, 0:128].reshape(LANES, 128)

    s_row = lax.broadcasted_iota(jnp.int32, (16, LANES), 0)
    s_col = lax.broadcasted_iota(jnp.int32, (16, LANES), 1)
    take = (lax.rem(s_col, 16) == 3) & (s_col // 64 == s_row)
    sums = jnp.dot(jnp.where(take, 1.0, 0.0).astype(BF16), rows, preferred_element_type=F32)
    target = target_of(ids_ref, slots_ref)
    result = jnp.zeros((8, TOK), F32)
    for e in range(EXP):
        for s in range(3):
            value = sums[e : e + 1, s : s + 1] + sums[e : e + 1, s + 8 : s + 9]
            result = jnp.where(target == e * 4 + s, value, result)
    prob_ref[...] = result


def shards(tokens, cotangent, expert_ids, slots, probs, w_gate, w_up, w_down):
    any_spec = pl.BlockSpec(memory_space=pl.ANY)
    vmem = pl.BlockSpec(memory_space=pltpu.VMEM)
    ring_sems = (MOST + 2) * 6
    ids_t, slots_t = expert_ids.T, slots.T
    rins_a, rins_b, spread = pl.pallas_call(
        kernel,
        out_shape=(
            jax.ShapeDtypeStruct((NP // 2, 16, CUTS[0][1]), BF16),
            jax.ShapeDtypeStruct((NP // 2, 16, CUTS[1][1]), BF16),
            jax.ShapeDtypeStruct((TOK, LANES), BF16),
        ),
        in_specs=[any_spec] * 8,
        out_specs=(any_spec, any_spec, any_spec),
        scratch_shapes=[
            pltpu.VMEM((8, TOK), jnp.int32),
            pltpu.VMEM((8, TOK), jnp.int32),
            pltpu.VMEM((8, TOK), BF16),
            pltpu.VMEM((TOK, LANES), BF16),
            pltpu.VMEM((2, 3, D, HID), BF16),
            pltpu.VMEM((TOK, D), BF16),
            pltpu.VMEM((TOK, D), BF16),
            pltpu.VMEM((EXP, 2, 16, QW), BF16),
            pltpu.VMEM((2, NP, 16, QW), BF16),
            pltpu.VMEM((2, NQ, ROWS, QW), BF16),
            pltpu.VMEM((3, ROWS, HID), F32),
            pltpu.VMEM((NQ, ROWS, QW), F32),
            pltpu.VMEM((NQ, ROWS // 2, CUTS[0][1]), BF16),
            pltpu.VMEM((NQ, ROWS // 2, CUTS[1][1]), BF16),
            pltpu.VMEM((NQ, ROWS // 2, CUTS[0][1]), BF16),
            pltpu.VMEM((NQ, ROWS // 2, CUTS[1][1]), BF16),
            pltpu.VMEM((NP // 2, 16, CUTS[0][1]), BF16),
            pltpu.VMEM((NP // 2, 16, CUTS[1][1]), BF16),
            pltpu.SemaphoreType.DMA((12,)),
            pltpu.SemaphoreType.DMA((ring_sems,)),
            pltpu.SemaphoreType.DMA((ring_sems,)),
            pltpu.SemaphoreType.DMA((ring_sems // 2,)),
            pltpu.SemaphoreType.DMA((ring_sems // 2,)),
            pltpu.SemaphoreType.DMA((NP,)),
            pltpu.SemaphoreType.DMA((NP,)),
            pltpu.SemaphoreType.DMA((2,)),
            pltpu.SemaphoreType.DMA((2,)),
            pltpu.SemaphoreType.DMA((NP,)),
            pltpu.SemaphoreType.DMA((NP,)),
            pltpu.SemaphoreType.REGULAR((4,)),
        ],
        compiler_params=pltpu.CompilerParams(
            collective_id=0, has_side_effects=True, vmem_limit_bytes=56 * 1024 * 1024
        ),
    )(tokens, cotangent, ids_t, slots_t, probs.T, w_gate, w_up, w_down.T)
    grad, prob_t = pl.pallas_call(
        combine,
        out_shape=(jax.ShapeDtypeStruct((TOK, D), BF16), jax.ShapeDtypeStruct((8, TOK), F32)),
        in_specs=[vmem] * 5,
        out_specs=(vmem, vmem),
    )(rins_a, rins_b, spread, ids_t, slots_t)
    return grad, prob_t.T


def solution(mesh):
    rows = P(("wide", "narrow"), None)
    in_specs = (rows, rows, rows, rows, rows, P("wide", "narrow"), P("wide", "narrow"), P("narrow", "wide"))
    return jax.shard_map(shards, mesh=mesh, in_specs=in_specs, out_specs=(rows, rows), check_vma=False)
```
